32 devices in a mesh: dp: 16 (over z, y, x), tensor: 2 (over core).
Axes of the slice: x: 2, y: 2, z: 4, core: 2. Of those that a mesh axis runs over, the one named last changes fastest.
Arguments:
- arrivals: bfloat16 [16384, 2048], P('dp', 'tensor')
- deal: int32 [16, 32], P('dp'), may hold values from 0 to 511, as said below
- seg_ids: int32 [16, 1024], P('dp'), may hold values from 0 to 7, never falling along the last dimension, each value on 1 to 512 neighbouring positions
- page_table: int32 [16, 8], P('dp'), may hold values from 0 to 7, each once within a row
- attn_gain: float32 [2048], replicated, may hold values from 0.1 to 1.9
- w_query: bfloat16 [2048, 1024], P(None, 'tensor'), may hold values from -0.125 to 0.125
- w_keyval: bfloat16 [2048, 512], replicated, may hold values from -0.125 to 0.125
- query_gain: float32 [64], replicated, may hold values from 0.1 to 1.9
- key_gain: float32 [64], replicated, may hold values from 0.1 to 1.9
- w_out: bfloat16 [1024, 2048], P('tensor'), may hold values from -0.1875 to 0.1875
- ffn_gain: float32 [2048], replicated, may hold values from 0.1 to 1.9
- w_gate: bfloat16 [2048, 5120], P(None, 'tensor'), may hold values from -0.125 to 0.125
- w_up: bfloat16 [2048, 5120], P(None, 'tensor'), may hold values from -0.125 to 0.125
- w_down: bfloat16 [5120, 2048], P('tensor'), may hold values from -0.078125 to 0.078125
Outputs:
- result: bfloat16 [16384, 2048], P('dp', 'tensor')
- kv_pages: bfloat16 [128, 128, 512], P('dp', None, 'tensor')
The draws below stay inside these ranges and needn't reach their ends.
Inputs may be any that keep to these rules, and one draw needn't show every extreme that they name: deal[s, k] = g * 32 + j sends unit k of arrival block s to unit j of group g; every value occurs once; the units of one arrival block go to exactly 16 groups, 2 units to each. `seg_ids`: each row never falls; one prompt is one run of equal numbers. `page_table`: each row holds every page number once.
All inputs are finite; a program needn't handle non-finite values.
Results may differ from the reference program's by a relative error of at most 0.019.
Values may be sent and summed in bfloat16 or wider, within the bound.
A program may use at most 128 MiB of HBM per device.

```python
import math
import jax
import jax.numpy as jnp
import numpy as np
from jax import lax

D = 2048
HEAD = 64
QH = 16
KVH = 4
FF = 5120
TOK_GRP = 1024
UNITS = 32
MOST = 2
PAGE = 128
SEGS = 8
UNIT = 32
PAGES = 8
GROUPS = 16
TOKENS = 16384
N_TENSOR = 2


def draw_arrivals(key, part):
    keys = jax.random.split(jax.random.fold_in(key, 3), 3)
    row_scale = jnp.exp(jax.random.uniform(keys[0], (TOKENS, 1), jnp.float32, math.log(0.5), math.log(1.5)))
    col_scale = jnp.exp(jax.random.uniform(keys[1], (1, D), jnp.float32, math.log(0.3), math.log(1.5)))
    base = jnp.clip(jax.random.normal(keys[2], (TOKENS, D), jnp.float32), -3.5, 3.5)
    return (base * row_scale * col_scale).astype(jnp.bfloat16)


def permute_units(key):
    return jax.random.permutation(key, UNITS)


def draw_deal(key, part):
    keys = jax.random.split(jax.random.fold_in(key, 7), 4)
    pairs = UNITS // MOST
    offsets = jax.random.permutation(keys[0], GROUPS)[:pairs]
    owners = jax.random.permutation(keys[1], GROUPS)
    orders = jax.vmap(permute_units)(jax.random.split(keys[2], GROUPS))
    places = jax.vmap(permute_units)(jax.random.split(keys[3], GROUPS))
    source = jnp.arange(GROUPS, dtype=jnp.int32)[:, None]
    target = owners[(source + offsets[orders // MOST]) % GROUPS]
    place = places[target, orders]
    return (target * UNITS + place).astype(jnp.int32)


def level_of(rng, dims, cuts, least, high):
    level = 1.0
    for dim, parts in cuts:
        steps = jax.random.uniform(jax.random.fold_in(jax.random.fold_in(rng, 6), dim), (parts,), jnp.float32, least / len(cuts), high / len(cuts))
        level = level * jnp.repeat(jnp.exp(steps), dims[dim] // parts).reshape((-1,) + (1,) * (len(dims) - 1 - dim))
    return level


def profile(number_of, total, limit, slope):
    weights = [(1 << 20) // math.isqrt(standing ** slope) + 1 for standing in range(2, number_of + 1)]
    spare, given = total - limit - (number_of - 1), [1] * (number_of - 1)
    while spare > 0:
        free = [i for i in range(number_of - 1) if given[i] < limit]
        mass, remaining = sum([weights[i] for i in free]), spare
        for i in free:
            more = min(limit - given[i], max(1, remaining * weights[i] // mass), spare)
            given[i] = given[i] + more
            spare = spare - more
    return np.array([limit] + given)


def uneven_parts(rng, count, total, limit, lean):
    if count == 2:
        one = jax.random.randint(rng, (), max(1, total - limit), min(limit, total - 1) + 1)
        return jnp.stack([one, total - one])
    tallies = jnp.asarray(profile(count, total, limit, lean), jnp.int32)
    twos = (count - 1) // 2
    giver, sink = tallies[1:1 + 2 * twos:2], tallies[2:2 + 2 * twos:2]
    slack = jnp.minimum(giver - 1, limit - sink)
    shifted = jax.random.randint(jax.random.fold_in(rng, 1), (twos,), 0, 1 << 20) % (slack + 1)
    tallies = tallies.at[1:1 + 2 * twos:2].set(giver - shifted).at[2:2 + 2 * twos:2].set(sink + shifted)
    return tallies[jax.random.permutation(jax.random.fold_in(rng, 2), count)]


def scatter_about(own_key, extent, scale, reach, cuts=(), kind=jnp.bfloat16):
    array = jax.random.normal(own_key, extent, jnp.float32) * scale
    if len(cuts) > 0:
        array = level_of(own_key, extent, cuts, -0.22, 0.18) * array
    return jnp.clip(array, min=-reach, max=reach).astype(kind)


def setup_inputs(seed: int = 0) -> dict:
    arg_keys = jax.random.split(jax.random.key(seed), 15)
    arrivals = draw_arrivals(jax.random.fold_in(arg_keys[14], 71), 0)
    deal = draw_deal(jax.random.fold_in(arg_keys[14], 71), 0)
    seg_ids = jax.vmap(lambda own: jnp.searchsorted(jnp.cumsum(uneven_parts(own, SEGS, TOK_GRP, TOK_GRP // 2, 2)), jnp.arange(TOK_GRP), side="right"))(jax.random.split(arg_keys[2], GROUPS)).reshape((GROUPS, TOK_GRP)).astype(jnp.int32)
    page_table = jax.vmap(lambda own: jax.random.permutation(own, PAGES))(jax.random.split(arg_keys[3], GROUPS)).reshape((GROUPS, PAGES)).astype(jnp.int32)
    attn_gain = jnp.clip(1.0 + 0.18 * jax.random.normal(arg_keys[4], (D,), jnp.float32), 0.1, 1.9)
    w_query = scatter_about(arg_keys[5], (D, QH * HEAD), D ** -0.5, 0.125, ((1, 2),))
    w_keyval = scatter_about(arg_keys[6], (D, 2 * KVH * HEAD), D ** -0.5, 0.125)
    query_gain = jnp.clip(1.0 + 0.18 * jax.random.normal(arg_keys[7], (HEAD,), jnp.float32), 0.1, 1.9)
    key_gain = jnp.clip(1.0 + 0.18 * jax.random.normal(arg_keys[8], (HEAD,), jnp.float32), 0.1, 1.9)
    w_out = scatter_about(arg_keys[9], (QH * HEAD, D), (QH * HEAD) ** -0.5, 0.1875, ((0, 2),))
    ffn_gain = jnp.clip(1.0 + 0.18 * jax.random.normal(arg_keys[10], (D,), jnp.float32), 0.1, 1.9)
    w_gate = scatter_about(arg_keys[11], (D, FF), D ** -0.5, 0.125, ((1, 2),))
    w_up = scatter_about(arg_keys[12], (D, FF), D ** -0.5, 0.125, ((1, 2),))
    w_down = scatter_about(arg_keys[13], (FF, D), FF ** -0.5, 0.078125, ((0, 2),))
    return dict(arrivals=arrivals, deal=deal, seg_ids=seg_ids, page_table=page_table, attn_gain=attn_gain, w_query=w_query, w_keyval=w_keyval, query_gain=query_gain, key_gain=key_gain, w_out=w_out, ffn_gain=ffn_gain, w_gate=w_gate, w_up=w_up, w_down=w_down)


EPS = 1e-06
THETA = 10000.0

def rms_scale(values, gain):
    values = values.astype(jnp.float32)
    mean_sq = lax.optimization_barrier(jnp.mean(values * values, axis=-1, keepdims=True))
    return values * lax.rsqrt(mean_sq + EPS) * gain.astype(jnp.float32)

def rope_tables(positions, width):
    half = width // 2
    inverse = THETA ** (-jnp.arange(half, dtype=jnp.float32) * 2.0 / width)
    angles = positions.astype(jnp.float32)[:, None] * inverse[None, :]
    return (jnp.cos(angles), jnp.sin(angles))

def rotate(values, cosine, sine):
    half = values.shape[-1] // 2
    first = values[..., :half]
    second = values[..., half:]
    cos_b = cosine[:, None, :]
    sin_b = sine[:, None, :]
    return jnp.concatenate([first * cos_b - second * sin_b, second * cos_b + first * sin_b], axis=-1)

def segment_starts(seg_row):
    count = seg_row.shape[0]
    index = jnp.arange(count, dtype=jnp.int32)
    prior = jnp.concatenate([seg_row[:1] - 1, seg_row[:-1]])
    marks = jnp.where(seg_row != prior, index, 0).astype(jnp.int32)
    return lax.cummax(marks, axis=0)

def partial_sum(left, right, blocks):
    width = left.shape[1] // blocks
    total = jnp.zeros((left.shape[0], right.shape[1]), jnp.float32)
    for block in range(blocks):
        term = jnp.dot(left[:, block * width:(block + 1) * width], right[block * width:(block + 1) * width], preferred_element_type=jnp.float32).astype(jnp.bfloat16)
        term = lax.optimization_barrier(term)
        total = total + term.astype(jnp.float32)
    return total

def reference(arrivals, deal, seg_ids, page_table, attn_gain, w_query, w_keyval, query_gain, key_gain, w_out, ffn_gain, w_gate, w_up, w_down):
    units_all = arrivals.reshape(GROUPS * UNITS, UNIT, D)
    slots = deal.reshape(-1).astype(jnp.int32)
    grouped = jnp.zeros_like(units_all).at[slots].set(units_all).reshape(GROUPS, TOK_GRP, D)

    def one_group(inputs):
        rows, seg_row, table = inputs
        normed = rms_scale(rows, attn_gain).astype(jnp.bfloat16)
        starts = segment_starts(seg_row)
        index = jnp.arange(TOK_GRP, dtype=jnp.int32)
        cosine, sine = rope_tables(index - starts, HEAD)
        q_raw = jnp.dot(normed, w_query, preferred_element_type=jnp.float32).reshape(TOK_GRP, QH, HEAD)
        queries = rotate(rms_scale(q_raw, query_gain), cosine, sine).astype(jnp.bfloat16)
        kv_raw = jnp.dot(normed, w_keyval, preferred_element_type=jnp.float32).reshape(TOK_GRP, KVH, 2, HEAD)
        keys = rotate(rms_scale(kv_raw[:, :, 0], key_gain), cosine, sine).astype(jnp.bfloat16)
        values = kv_raw[:, :, 1].astype(jnp.bfloat16)
        cache = jnp.stack([keys, values], axis=2).reshape(PAGES, PAGE, KVH * 2 * HEAD)
        cache = jnp.zeros_like(cache).at[table.astype(jnp.int32)].set(cache)
        q_grouped = queries.astype(jnp.float32).reshape(TOK_GRP, KVH, QH // KVH, HEAD)
        scores = jnp.einsum('ikgd,jkd->kgij', q_grouped, keys.astype(jnp.float32)) * (1.0 / math.sqrt(HEAD))
        allowed = jnp.logical_and(index[:, None] >= index[None, :], starts[:, None] <= index[None, :])
        weights = jnp.where(allowed, jnp.exp(scores), 0.0)
        probs = (weights / lax.optimization_barrier(jnp.sum(weights, axis=-1, keepdims=True))).astype(jnp.bfloat16)
        attended = jnp.einsum('kgij,jkd->ikgd', probs.astype(jnp.float32), values.astype(jnp.float32))
        attended = attended.astype(jnp.bfloat16).reshape(TOK_GRP, QH * HEAD)
        middle = (rows.astype(jnp.float32) + partial_sum(attended, w_out, N_TENSOR)).astype(jnp.bfloat16)
        ffn_in = rms_scale(middle, ffn_gain).astype(jnp.bfloat16)
        gate = jnp.dot(ffn_in, w_gate, preferred_element_type=jnp.float32)
        upper = jnp.dot(ffn_in, w_up, preferred_element_type=jnp.float32)
        hidden = (jax.nn.silu(gate) * upper).astype(jnp.bfloat16)
        combined = (middle.astype(jnp.float32) + partial_sum(hidden, w_down, N_TENSOR)).astype(jnp.bfloat16)
        return (combined, cache)
    combined, caches = lax.map(one_group, (grouped, seg_ids, page_table))
    back = combined.reshape(GROUPS * UNITS, UNIT, D)[slots]
    return (back.reshape(TOKENS, D), caches.reshape(GROUPS * PAGES, PAGE, KVH * 2 * HEAD))
```

```python
import functools
import math

import jax
import jax.numpy as jnp
from jax import lax
from jax.experimental import pallas as pl
from jax.experimental.pallas import tpu as pltpu
from jax.sharding import PartitionSpec as P

HEAD = 64
KVH = 4
MOST = 2
PAGE = 128
WINDOW = 512
EPS = 1e-06
THETA = 10000.0
LANES = 128
TILE = 256
VMEM_LIMIT = 60 * 1024 * 1024

VMEM = pl.BlockSpec(memory_space=pltpu.VMEM)
SMEM = pl.BlockSpec(memory_space=pltpu.SMEM)


def segment_starts(seg_row):
    count = seg_row.shape[0]
    index = jnp.arange(count, dtype=jnp.int32)
    prior = jnp.concatenate([seg_row[:1] - 1, seg_row[:-1]])
    marks = jnp.where(seg_row != prior, index, 0)
    return lax.cummax(marks, axis=0)


def qkv_kernel(unit_rows, slots, src, x, gain, wq, wkv, hgain, normed_cols, mean_mat, out, held):
    step = pl.program_id(0)
    rows = x.shape[0]
    qcols = wq.shape[1]
    cols = qcols + wkv.shape[1]
    xv = x[...].astype(jnp.float32)
    ms = jnp.mean(xv * xv, axis=-1, keepdims=True)
    xn = (xv * lax.rsqrt(ms + EPS) * gain[...]).astype(jnp.bfloat16)
    q = jnp.dot(xn, wq[...], preferred_element_type=jnp.float32)
    kv = jnp.dot(xn, wkv[...], preferred_element_type=jnp.float32)
    here = pl.ds(pl.multiple_of(step * rows, rows), rows)
    for first in range(0, cols, LANES):
        if first < qcols:
            part = q[:, first : first + LANES]
        else:
            part = kv[:, first - qcols : first - qcols + LANES]
        mean = jnp.dot(
            (part * part).astype(jnp.bfloat16), mean_mat[...], preferred_element_type=jnp.float32
        )
        at = slice(first, first + LANES)
        scaled = part * lax.rsqrt(mean + EPS) * hgain[:, at]
        held[here, at] = jnp.where(normed_cols[:, at] > 0.5, scaled, part).astype(jnp.bfloat16)

    @pl.when(step == pl.num_programs(0) - 1)
    def _():
        def move(slot, carry):
            frm = pl.multiple_of(src[slot] * unit_rows, unit_rows)
            to = pl.multiple_of(slot * unit_rows, unit_rows)
            out[pl.ds(to, unit_rows), :] = held[pl.ds(frm, unit_rows), :]
            return carry

        lax.fori_loop(0, slots, move, 0)


def attention_kernel(
    unit_rows, slots, qcols, slot_of, pos_of, table, recv, cosq, sinq, coskv, sinkv, starts, rot,
    pages, back, got, qs, kvs, att
):
    tokens, cols = got.shape
    units = tokens // unit_rows

    def fetch(unit, carry):
        frm = pl.multiple_of(slot_of[unit] * unit_rows, unit_rows)
        to = pl.multiple_of(unit * unit_rows, unit_rows)
        got[pl.ds(to, unit_rows), :] = recv[pl.ds(frm, unit_rows), :]
        return carry

    lax.fori_loop(0, units, fetch, 0)
    scale = math.log2(math.e) / math.sqrt(HEAD)
    for first in range(0, cols, LANES):
        at = slice(first, first + LANES)
        part = got[:, at]
        turned = jnp.dot(part, rot[...], preferred_element_type=jnp.float32)
        part = part.astype(jnp.float32)
        if first < qcols:
            qs[:, at] = ((part * cosq[...] + turned * sinq[...]) * scale).astype(jnp.bfloat16)
        else:
            kvs[:, first - qcols : first - qcols + LANES] = (
                part * coskv[...] + turned * sinkv[...]
            ).astype(jnp.bfloat16)
    page_rows = pages.shape[1]

    def page(p, carry):
        pages[table[p], :, :] = kvs[pl.ds(pl.multiple_of(p * page_rows, page_rows), page_rows), :]
        return carry

    lax.fori_loop(0, pages.shape[0], page, 0)

    kv_heads = kvs.shape[1] // LANES
    pairs = qcols // LANES // kv_heads
    low = lax.broadcasted_iota(jnp.int32, (1, LANES), 1) < HEAD
    for head in range(kv_heads):
        kv = kvs[:, head * LANES : (head + 1) * LANES].astype(jnp.float32)
        kvr = pltpu.roll(kv, HEAD, 1)
        key_e = kv.astype(jnp.bfloat16)
        key_o = kvr.astype(jnp.bfloat16)
        val_e = jnp.where(low, kvr, 1.0).astype(jnp.bfloat16)
        val_o = jnp.where(low, 1.0, kv).astype(jnp.bfloat16)
        for i0 in range(0, tokens, TILE):
            j0 = max(0, i0 - WINDOW)
            i1 = i0 + TILE
            rows = lax.broadcasted_iota(jnp.int32, (TILE, i1 - j0), 0) + i0
            keys = lax.broadcasted_iota(jnp.int32, (TILE, i1 - j0), 1) + j0
            allowed = jnp.logical_and(rows >= keys, starts[i0:i1, :] <= keys)
            bias = jnp.where(allowed, 0.0, -1e30)
            for pair in range(pairs):
                at = slice((head * pairs + pair) * LANES, (head * pairs + pair + 1) * LANES)
                q = qs[i0:i1, at]
                outs = []
                for keep, key, val in ((low, key_e, val_e), (jnp.logical_not(low), key_o, val_o)):
                    qm = jnp.where(keep, q, jnp.zeros_like(q))
                    s = lax.dot_general(
                        qm, key[j0:i1], (((1,), (1,)), ((), ())), preferred_element_type=jnp.float32
                    )
                    w = jnp.exp2(s + bias).astype(jnp.bfloat16)
                    outs.append(jnp.dot(w, val[j0:i1], preferred_element_type=jnp.float32))
                even, odd = outs
                den = pltpu.roll(jnp.where(low, odd, even), HEAD, 1)
                att[i0:i1, at] = (jnp.where(low, even, odd) / den).astype(jnp.bfloat16)

    def give(slot, carry):
        frm = pl.multiple_of(pos_of[slot] * unit_rows, unit_rows)
        to = pl.multiple_of(slot * unit_rows, unit_rows)
        back[pl.ds(to, unit_rows), :] = att[pl.ds(frm, unit_rows), :]
        return carry

    lax.fori_loop(0, slots, give, 0)


def gather_kernel(unit_rows, slot_of, came, out):
    def fetch(unit, carry):
        frm = pl.multiple_of(slot_of[unit] * unit_rows, unit_rows)
        to = pl.multiple_of(unit * unit_rows, unit_rows)
        out[pl.ds(to, unit_rows), :] = came[pl.ds(frm, unit_rows), :]
        return carry

    lax.fori_loop(0, out.shape[0] // unit_rows, fetch, 0)


def ffn_kernel(
    nf, rank, x, att, wo, gain, wg, wu, wd, part, mid, ffn_in, hidden
):
    step = pl.program_id(0)
    tokens = x.shape[0]
    fp = mid.shape[1]
    ft = wg.shape[1]

    @pl.when(step == 0)
    def _():
        own = pl.ds(pl.multiple_of(rank[0] * fp, fp), fp)

        def rows(i, carry):
            at = pl.ds(pl.multiple_of(i * TILE, TILE), TILE)
            total = jnp.dot(att[at, :], wo[...], preferred_element_type=jnp.float32)
            middle = (x[at, :].astype(jnp.float32) + total).astype(jnp.bfloat16)
            ffn_in[at, :] = middle
            mid[at, :] = ffn_in[at, own]
            m = middle.astype(jnp.float32)
            ms = jnp.mean(m * m, axis=-1, keepdims=True)
            ffn_in[at, :] = (m * lax.rsqrt(ms + EPS) * gain[...]).astype(jnp.bfloat16)
            return carry

        lax.fori_loop(0, tokens // TILE, rows, 0)

    @pl.when(step < nf)
    def _():
        cols = pl.ds(pl.multiple_of(step * ft, ft), ft)

        def rows(i, carry):
            at = pl.ds(pl.multiple_of(i * TILE, TILE), TILE)
            g = jnp.dot(ffn_in[at, :], wg[...], preferred_element_type=jnp.float32)
            u = jnp.dot(ffn_in[at, :], wu[...], preferred_element_type=jnp.float32)
            hidden[at, cols] = (g / (1.0 + jnp.exp(-g)) * u).astype(jnp.bfloat16)
            return carry

        lax.fori_loop(0, tokens // TILE, rows, 0)

    @pl.when(step >= nf)
    def _():
        def rows(i, carry):
            at = pl.ds(pl.multiple_of(i * TILE, TILE), TILE)
            part[at, :] = jnp.dot(
                hidden[at, :], wd[...], preferred_element_type=jnp.float32
            ).astype(jnp.bfloat16)
            return carry

        lax.fori_loop(0, tokens // TILE, rows, 0)


def on_device(
    arrivals, deal, seg_ids, page_table, attn_gain, w_query, w_keyval, query_gain, key_gain,
    w_out, ffn_gain, w_gate, w_up, w_down,
):
    groups = lax.axis_size("dp")
    shards = lax.axis_size("tensor")
    me = lax.axis_index("dp")
    rank_t = lax.axis_index("tensor")
    tokens, fp = arrivals.shape
    units = deal.shape[1]
    unit_rows = tokens // units
    slots = groups * MOST
    width = fp * shards
    qcols = w_query.shape[1]
    kv_heads = max(1, KVH // shards)
    kv_first = rank_t * KVH // shards
    cache_cols = 2 * KVH * HEAD // shards
    kvcols = 2 * HEAD * kv_heads
    cols = qcols + kvcols
    params = pltpu.CompilerParams(vmem_limit_bytes=VMEM_LIMIT)

    full = lax.all_gather(arrivals, "tensor", axis=1, tiled=True)
    deal_all = lax.all_gather(deal[0], "dp", axis=0)
    wo_full = lax.all_gather(w_out, "tensor", axis=0, tiled=True)

    dest_row = deal[0]
    target = dest_row // units
    unit_index = jnp.arange(units, dtype=jnp.int32)
    earlier = unit_index[:, None] > unit_index[None, :]
    rank = jnp.sum(jnp.logical_and(earlier, target[:, None] == target[None, :]), axis=1)
    slot = (target * MOST + rank).astype(jnp.int32)
    slot_index = jnp.arange(slots, dtype=jnp.int32)
    hot = slot[None, :] == slot_index[:, None]
    src = jnp.sum(jnp.where(hot, unit_index[None, :], 0), axis=1).astype(jnp.int32)

    mine = deal_all // units == me
    place = deal_all % units
    before = jnp.sum(
        jnp.logical_and(earlier[None], mine[:, None, :]).astype(jnp.int32), axis=2
    )
    sel = jnp.logical_and(
        mine[:, None, :], before[:, None, :] == jnp.arange(MOST, dtype=jnp.int32)[None, :, None]
    )
    recv_pos = jnp.sum(jnp.where(sel, place[:, None, :] + 1, 0), axis=2).reshape(-1) - 1
    fill = recv_pos[None, :] == unit_index[:, None]
    slot_of = jnp.sum(jnp.where(fill, slot_index[None, :], 0), axis=1).astype(jnp.int32)
    pos_of = jnp.maximum(recv_pos, 0).astype(jnp.int32)

    kv_weight = lax.dynamic_slice_in_dim(w_keyval, kv_first * 2 * HEAD, kvcols, 1)
    ones = jnp.ones((HEAD,), jnp.float32)
    hgain = jnp.concatenate(
        [jnp.tile(query_gain, qcols // HEAD)]
        + [jnp.concatenate([key_gain, ones])] * kv_heads
    )[None, :]
    normed_cols = jnp.concatenate(
        [jnp.ones((qcols,), jnp.float32)]
        + [jnp.concatenate([ones, jnp.zeros((HEAD,), jnp.float32)])] * kv_heads
    )[None, :]
    lane = jnp.arange(LANES, dtype=jnp.int32)
    mean_mat = jnp.where(
        lane[:, None] // HEAD == lane[None, :] // HEAD, 1.0 / HEAD, 0.0
    ).astype(jnp.bfloat16)

    const = lambda shape: pl.BlockSpec(
        shape, lambda i: (0,) * len(shape), pipeline_mode=pl.Buffered(1)
    )
    packed = pl.pallas_call(
        functools.partial(qkv_kernel, unit_rows, slots),
        grid=(tokens // TILE,),
        in_specs=[
            SMEM,
            pl.BlockSpec((TILE, width), lambda i: (i, 0)),
            const((1, width)),
            const((width, qcols)),
            const((width, kvcols)),
            const((1, cols)),
            const((1, cols)),
            const((LANES, LANES)),
        ],
        out_specs=pl.BlockSpec((slots * unit_rows, cols), lambda i: (0, 0)),
        out_shape=jax.ShapeDtypeStruct((slots * unit_rows, cols), jnp.bfloat16),
        scratch_shapes=[pltpu.VMEM((tokens, cols), jnp.bfloat16)],
        compiler_params=params,
        name="qkv",
    )(src, full, attn_gain[None, :], w_query, kv_weight, hgain, normed_cols, mean_mat)

    received = lax.all_to_all(
        packed.reshape(groups, MOST * unit_rows, cols), "dp", split_axis=0, concat_axis=0, tiled=True
    ).reshape(slots * unit_rows, cols)

    starts = segment_starts(seg_ids[0])
    half = HEAD // 2
    inverse = THETA ** (-jnp.arange(half, dtype=jnp.float32) * 2.0 / HEAD)
    positions = jnp.arange(tokens, dtype=jnp.int32) - starts
    angles = positions.astype(jnp.float32)[:, None] * inverse[None, :]
    cosine, sine = jnp.cos(angles), jnp.sin(angles)
    cosq = jnp.tile(cosine, (1, 4))
    sinq = jnp.tile(sine, (1, 4))
    coskv = jnp.concatenate([cosine, cosine, jnp.ones((tokens, HEAD), jnp.float32)], axis=1)
    sinkv = jnp.concatenate([sine, sine, jnp.zeros((tokens, HEAD), jnp.float32)], axis=1)
    inn, out_l = lane[:, None], lane[None, :]
    rot = jnp.where(
        jnp.logical_and(out_l % HEAD < half, inn == out_l + half),
        -1.0,
        jnp.where(jnp.logical_and(out_l % HEAD >= half, inn == out_l - half), 1.0, 0.0),
    ).astype(jnp.bfloat16)

    npages = tokens // PAGE
    kv_pages, back = pl.pallas_call(
        functools.partial(attention_kernel, unit_rows, slots, qcols),
        in_specs=[SMEM] * 3 + [VMEM] * 7,
        out_specs=[VMEM] * 2,
        out_shape=[
            jax.ShapeDtypeStruct((npages, PAGE, kvcols), jnp.bfloat16),
            jax.ShapeDtypeStruct((slots * unit_rows, qcols), jnp.bfloat16),
        ],
        scratch_shapes=[
            pltpu.VMEM((tokens, cols), jnp.bfloat16),
            pltpu.VMEM((tokens, qcols), jnp.bfloat16),
            pltpu.VMEM((tokens, kvcols), jnp.bfloat16),
            pltpu.VMEM((tokens, qcols), jnp.bfloat16),
        ],
        compiler_params=params,
        name="attention",
    )(slot_of, pos_of, page_table[0], received, cosq, sinq, coskv, sinkv, starts[:, None], rot)

    if cache_cols < kvcols:
        offset = rank_t * cache_cols - kv_first * 2 * HEAD
        kv_pages = lax.dynamic_slice_in_dim(kv_pages, offset, cache_cols, 2)

    returned = lax.all_to_all(
        back.reshape(groups, MOST * unit_rows, qcols), "dp", split_axis=0, concat_axis=0, tiled=True
    ).reshape(slots * unit_rows, qcols)
    att = pl.pallas_call(
        functools.partial(gather_kernel, unit_rows),
        in_specs=[SMEM, VMEM],
        out_specs=VMEM,
        out_shape=jax.ShapeDtypeStruct((tokens, qcols), jnp.bfloat16),
        compiler_params=params,
        name="ungroup",
    )(slot, returned)
    att_full = lax.all_gather(att, "tensor", axis=1, tiled=True)

    ff = w_gate.shape[1]
    ft = next(t for t in (512, 256, 128) if ff % t == 0)
    dt = 512
    nf, nd = ff // ft, width // dt
    part, mid = pl.pallas_call(
        functools.partial(ffn_kernel, nf),
        grid=(nf + nd,),
        in_specs=[
            SMEM,
            const((tokens, width)),
            const((tokens, qcols * shards)),
            const((qcols * shards, width)),
            const((1, width)),
            pl.BlockSpec((width, ft), lambda i: (0, jnp.minimum(i, nf - 1))),
            pl.BlockSpec((width, ft), lambda i: (0, jnp.minimum(i, nf - 1))),
            pl.BlockSpec((ff, dt), lambda i: (0, jnp.maximum(i - nf, 0))),
        ],
        out_specs=[
            pl.BlockSpec((tokens, dt), lambda i: (0, jnp.maximum(i - nf, 0))),
            pl.BlockSpec((tokens, fp), lambda i: (0, 0)),
        ],
        out_shape=[
            jax.ShapeDtypeStruct((tokens, width), jnp.bfloat16),
            jax.ShapeDtypeStruct((tokens, fp), jnp.bfloat16),
        ],
        scratch_shapes=[
            pltpu.VMEM((tokens, width), jnp.bfloat16),
            pltpu.VMEM((tokens, ff), jnp.bfloat16),
        ],
        compiler_params=params,
        name="ffn",
    )(
        rank_t.astype(jnp.int32)[None], full, att_full, wo_full, ffn_gain[None, :],
        w_gate, w_up, w_down,
    )
    summed = lax.psum_scatter(part, "tensor", scatter_dimension=1, tiled=True)
    result = (mid.astype(jnp.float32) + summed.astype(jnp.float32)).astype(jnp.bfloat16)
    return (result, kv_pages)


def solution(mesh):
    return jax.shard_map(
        on_device,
        mesh=mesh,
        in_specs=(
            P("dp", "tensor"),
            P("dp", None),
            P("dp", None),
            P("dp", None),
            P(),
            P(None, "tensor"),
            P(),
            P(),
            P(),
            P("tensor", None),
            P(),
            P(None, "tensor"),
            P(None, "tensor"),
            P("tensor", None),
        ),
        out_specs=(P("dp", "tensor"), P("dp", None, "tensor")),
        check_vma=False,
    )
```

```python
import functools
import math

import jax
import jax.numpy as jnp
from jax import lax
from jax.experimental import pallas as pl
from jax.experimental.pallas import tpu as pltpu
from jax.sharding import PartitionSpec as P

HEAD = 64
KVH = 4
MOST = 2
PAGE = 128
WINDOW = 512
EPS = 1e-06
THETA = 10000.0
LANES = 128
TILE = 256
ROWS = 512
MESH = pl.DeviceIdType.MESH
VMEM_LIMIT = 60 * 1024 * 1024

VMEM = pl.BlockSpec(memory_space=pltpu.VMEM)
ANY = pl.BlockSpec(memory_space=pl.ANY)
SMEM = pl.BlockSpec(memory_space=pltpu.SMEM)


def segment_starts(seg_row):
    count = seg_row.shape[0]
    index = jnp.arange(count, dtype=jnp.int32)
    prior = jnp.concatenate([seg_row[:1] - 1, seg_row[:-1]])
    marks = jnp.where(seg_row != prior, index, 0)
    return lax.cummax(marks, axis=0)


def greet(peers):
    barrier = pltpu.get_barrier_semaphore()
    for peer in peers:
        pl.semaphore_signal(barrier, inc=1, device_id=peer, device_id_type=MESH)
    pl.semaphore_wait(barrier, len(peers))


def qkv_kernel(
    groups, shards, pos, x, gain, wq_hbm, wkv_hbm, hgain, normed_cols,
    mean_mat, held, xg, rpos, xn, wq, wkv, wsem, lsem, xsend, xrecv, psend, precv
):
    me, rank = lax.axis_index("dp"), lax.axis_index("tensor")
    tokens, fp = x.shape
    qcols, kvcols = wq.shape[1], wkv.shape[1]
    cols = qcols + kvcols
    chunks = tokens // TILE
    kv_at = pl.multiple_of((rank * KVH // shards) * 2 * HEAD, 2 * HEAD)
    loads = [
        pltpu.make_async_copy(wq_hbm, wq, wsem.at[0]),
        pltpu.make_async_copy(wkv_hbm.at[:, pl.ds(kv_at, kvcols)], wkv, wsem.at[1]),
    ]
    local = [
        pltpu.make_async_copy(
            x.at[c * TILE : (c + 1) * TILE, :],
            xg.at[rank, c * TILE : (c + 1) * TILE, :],
            lsem.at[c],
        )
        for c in range(chunks)
    ]
    for copy in local + loads:
        copy.start()
    greet(
        [{"dp": lax.rem(me + d, groups)} for d in range(1, groups)]
        + [{"tensor": lax.rem(rank + d, shards)} for d in range(1, shards)]
    )
    swaps = [
        [
            pltpu.make_async_remote_copy(
                src_ref=x.at[c * TILE : (c + 1) * TILE, :],
                dst_ref=xg.at[rank, c * TILE : (c + 1) * TILE, :],
                send_sem=xsend.at[d - 1, c],
                recv_sem=xrecv.at[d - 1, c],
                device_id={"tensor": lax.rem(rank + d, shards)},
                device_id_type=MESH,
            )
            for d in range(1, shards)
        ]
        for c in range(chunks)
    ]
    for row in swaps:
        for copy in row:
            copy.start()
    places = []
    for d in range(1, groups):
        to = lax.rem(me + d, groups)
        places.append(
            pltpu.make_async_remote_copy(
                src_ref=pos.at[to],
                dst_ref=rpos.at[me],
                send_sem=psend.at[d - 1],
                recv_sem=precv.at[d - 1],
                device_id={"dp": to},
                device_id_type=MESH,
            )
        )
    for copy in places:
        copy.start()
    rpos[me] = pos[me]
    for c in range(chunks):
        here = slice(c * TILE, (c + 1) * TILE)
        local[c].wait()
        for copy in swaps[c]:
            copy.wait_recv()
        total = jnp.zeros((TILE, 1), jnp.float32)
        for t in range(shards):
            xv = xg[t, here, :].astype(jnp.float32)
            total += jnp.sum(xv * xv, axis=-1, keepdims=True)
        inv = lax.rsqrt(total / (fp * shards) + EPS)
        for t in range(shards):
            at = slice(t * fp, (t + 1) * fp)
            xv = xg[t, here, :].astype(jnp.float32)
            xn[:, at] = (xv * inv * gain[:, at]).astype(jnp.bfloat16)
        if c == 0:
            for copy in loads:
                copy.wait()
        q = jnp.dot(xn[...], wq[...], preferred_element_type=jnp.float32)
        kv = jnp.dot(xn[...], wkv[...], preferred_element_type=jnp.float32)
        for first in range(0, cols, LANES):
            if first < qcols:
                part = q[:, first : first + LANES]
            else:
                part = kv[:, first - qcols : first - qcols + LANES]
            mean = jnp.dot(
                (part * part).astype(jnp.bfloat16), mean_mat[...], preferred_element_type=jnp.float32
            )
            at = slice(first, first + LANES)
            scaled = part * lax.rsqrt(mean + EPS) * hgain[:, at]
            held[here, at] = jnp.where(normed_cols[:, at] > 0.5, scaled, part).astype(jnp.bfloat16)

    for row in swaps:
        for copy in row:
            copy.wait_send()
    for copy in places:
        copy.wait()


def attention_kernel(
    unit_rows, slots, qcols, slot_of, pos_of, table, recv, cosq, sinq, coskv, sinkv, starts, rot,
    pages, back, got, qs, kvs, att
):
    tokens, cols = got.shape
    units = tokens // unit_rows

    def fetch(unit, carry):
        frm = pl.multiple_of(slot_of[unit] * unit_rows, unit_rows)
        to = pl.multiple_of(unit * unit_rows, unit_rows)
        got[pl.ds(to, unit_rows), :] = recv[pl.ds(frm, unit_rows), :]
        return carry

    lax.fori_loop(0, units, fetch, 0)
    scale = math.log2(math.e) / math.sqrt(HEAD)
    for first in range(0, cols, LANES):
        at = slice(first, first + LANES)
        part = got[:, at]
        turned = jnp.dot(part, rot[...], preferred_element_type=jnp.float32)
        part = part.astype(jnp.float32)
        if first < qcols:
            qs[:, at] = ((part * cosq[...] + turned * sinq[...]) * scale).astype(jnp.bfloat16)
        else:
            kvs[:, first - qcols : first - qcols + LANES] = (
                part * coskv[...] + turned * sinkv[...]
            ).astype(jnp.bfloat16)
    page_rows = pages.shape[1]

    def page(p, carry):
        pages[table[p], :, :] = kvs[pl.ds(pl.multiple_of(p * page_rows, page_rows), page_rows), :]
        return carry

    lax.fori_loop(0, pages.shape[0], page, 0)

    kv_heads = kvs.shape[1] // LANES
    pairs = qcols // LANES // kv_heads
    low = lax.broadcasted_iota(jnp.int32, (1, LANES), 1) < HEAD
    for head in range(kv_heads):
        kv = kvs[:, head * LANES : (head + 1) * LANES].astype(jnp.float32)
        kvr = pltpu.roll(kv, HEAD, 1)
        key_e = kv.astype(jnp.bfloat16)
        key_o = kvr.astype(jnp.bfloat16)
        val_e = jnp.where(low, kvr, 1.0).astype(jnp.bfloat16)
        val_o = jnp.where(low, 1.0, kv).astype(jnp.bfloat16)
        for i0 in range(0, tokens, TILE):
            j0 = max(0, i0 - WINDOW)
            i1 = i0 + TILE
            rows = lax.broadcasted_iota(jnp.int32, (TILE, i1 - j0), 0) + i0
            keys = lax.broadcasted_iota(jnp.int32, (TILE, i1 - j0), 1) + j0
            allowed = jnp.logical_and(rows >= keys, starts[i0:i1, :] <= keys)
            bias = jnp.where(allowed, 0.0, -1e30)
            for pair in range(pairs):
                at = slice((head * pairs + pair) * LANES, (head * pairs + pair + 1) * LANES)
                q = qs[i0:i1, at]
                outs = []
                for keep, key, val in ((low, key_e, val_e), (jnp.logical_not(low), key_o, val_o)):
                    qm = jnp.where(keep, q, jnp.zeros_like(q))
                    s = lax.dot_general(
                        qm, key[j0:i1], (((1,), (1,)), ((), ())), preferred_element_type=jnp.float32
                    )
                    w = jnp.exp2(s + bias).astype(jnp.bfloat16)
                    outs.append(jnp.dot(w, val[j0:i1], preferred_element_type=jnp.float32))
                even, odd = outs
                den = pltpu.roll(jnp.where(low, odd, even), HEAD, 1)
                att[i0:i1, at] = (jnp.where(low, even, odd) / den).astype(jnp.bfloat16)

    def give(slot, carry):
        frm = pl.multiple_of(pos_of[slot] * unit_rows, unit_rows)
        to = pl.multiple_of(slot * unit_rows, unit_rows)
        back[pl.ds(to, unit_rows), :] = att[pl.ds(frm, unit_rows), :]
        return carry

    lax.fori_loop(0, slots, give, 0)


def move_kernel(unit_rows, source_of, came, out):
    def move(unit, carry):
        frm = pl.multiple_of(source_of[unit] * unit_rows, unit_rows)
        to = pl.multiple_of(unit * unit_rows, unit_rows)
        out[pl.ds(to, unit_rows), :] = came[pl.ds(frm, unit_rows), :]
        return carry

    lax.fori_loop(0, out.shape[0] // unit_rows, move, 0)


def move_units(source_of, came, units, unit_rows):
    return pl.pallas_call(
        functools.partial(move_kernel, unit_rows),
        in_specs=[SMEM, VMEM],
        out_specs=VMEM,
        out_shape=jax.ShapeDtypeStruct((units * unit_rows, came.shape[1]), came.dtype),
        compiler_params=pltpu.CompilerParams(vmem_limit_bytes=VMEM_LIMIT),
        name="move_units",
    )(source_of, came)


def ffn_kernel(
    nf, shards, xg, came, wo, gain, wg, wu, wd_hbm, out, att, mid, ffn_in,
    hidden, wd, sbuf, rbuf, wsem, asend, arecv, csend, crecv
):
    step = pl.program_id(0)
    rank = lax.axis_index("tensor")
    tokens, fp = mid.shape
    qcols = came.shape[1]
    ft = wg.shape[1]
    dt = wd.shape[2]
    per = fp // dt
    nd = per * shards
    chunks = tokens // TILE

    loads = []
    for d in range(nd):
        column = lax.rem(rank + 1 + d // per, shards) * fp + (d % per) * dt
        loads.append(
            pltpu.make_async_copy(
                wd_hbm.at[:, pl.ds(pl.multiple_of(column, dt), dt)], wd.at[d], wsem.at[d]
            )
        )
    swaps = [
        [
            pltpu.make_async_remote_copy(
                src_ref=att.at[rank, c * TILE : (c + 1) * TILE, :],
                dst_ref=att.at[rank, c * TILE : (c + 1) * TILE, :],
                send_sem=asend.at[d - 1, c],
                recv_sem=arecv.at[d - 1, c],
                device_id={"tensor": lax.rem(rank + d, shards)},
                device_id_type=MESH,
            )
            for d in range(1, shards)
        ]
        for c in range(chunks)
    ]
    shares = [
        pltpu.make_async_remote_copy(
            src_ref=sbuf.at[d],
            dst_ref=rbuf.at[d],
            send_sem=csend.at[d],
            recv_sem=crecv.at[d],
            device_id={"tensor": lax.rem(rank + 1 + d // per, shards)},
            device_id_type=MESH,
        )
        for d in range(nd - per)
    ]

    @pl.when(step == 0)
    def _():
        greet([{"tensor": lax.rem(rank + d, shards)} for d in range(1, shards)])
        for c in range(chunks):
            here = slice(c * TILE, (c + 1) * TILE)
            att[rank, here, :] = came[here, :]
            for copy in swaps[c]:
                copy.start()
        for copy in loads:
            copy.start()
        for c in range(chunks):
            here = slice(c * TILE, (c + 1) * TILE)
            for copy in swaps[c]:
                copy.wait_recv()
            total = jnp.dot(
                att[0, here, :], wo[0:qcols, :], preferred_element_type=jnp.float32
            )
            for t in range(1, shards):
                total += jnp.dot(
                    att[t, here, :],
                    wo[t * qcols : (t + 1) * qcols, :],
                    preferred_element_type=jnp.float32,
                )
            square = jnp.zeros((TILE, 1), jnp.float32)
            for t in range(shards):
                at = slice(t * fp, (t + 1) * fp)
                m = (xg[t, here, :].astype(jnp.float32) + total[:, at]).astype(jnp.bfloat16)
                ffn_in[here, at] = m
                m = m.astype(jnp.float32)
                square += jnp.sum(m * m, axis=-1, keepdims=True)
            mid[here, :] = ffn_in[here, pl.ds(pl.multiple_of(rank * fp, fp), fp)]
            inv = lax.rsqrt(square / (fp * shards) + EPS)
            for t in range(shards):
                at = slice(t * fp, (t + 1) * fp)
                m = ffn_in[here, at].astype(jnp.float32)
                ffn_in[here, at] = (m * inv * gain[:, at]).astype(jnp.bfloat16)
        for row in swaps:
            for copy in row:
                copy.wait_send()

    @pl.when(step < nf)
    def _():
        cols = pl.ds(pl.multiple_of(step * ft, ft), ft)

        def rows(i, carry):
            at = pl.ds(pl.multiple_of(i * ROWS, ROWS), ROWS)
            g = jnp.dot(ffn_in[at, :], wg[...], preferred_element_type=jnp.float32)
            u = jnp.dot(ffn_in[at, :], wu[...], preferred_element_type=jnp.float32)
            hidden[at, cols] = (g / (1.0 + jnp.exp(-g)) * u).astype(jnp.bfloat16)
            return carry

        lax.fori_loop(0, tokens // ROWS, rows, 0)

    for d in range(nd):
        @pl.when(step == nf + d)
        def _(d=d):
            loads[d].wait()
            j = d - (nd - per)
            cols = slice(j * dt, (j + 1) * dt)
            if j >= 0:
                for k in range(shards - 1):
                    shares[k * per + j].wait_recv()

            def rows(i, carry):
                at = pl.ds(pl.multiple_of(i * ROWS, ROWS), ROWS)
                part = jnp.dot(hidden[at, :], wd[d], preferred_element_type=jnp.float32)
                if j < 0:
                    sbuf[d, at, :] = part.astype(jnp.bfloat16)
                else:
                    for k in range(shards - 1):
                        part += rbuf[k * per + j, at, :].astype(jnp.float32)
                    out[at, cols] = (mid[at, cols].astype(jnp.float32) + part).astype(jnp.bfloat16)
                return carry

            lax.fori_loop(0, tokens // ROWS, rows, 0)
            if j < 0:
                shares[d].start()
            if d == nd - 1:
                for copy in shares:
                    copy.wait_send()


def on_device(
    arrivals, deal, seg_ids, page_table, attn_gain, w_query, w_keyval, query_gain, key_gain,
    w_out, ffn_gain, w_gate, w_up, w_down,
):
    groups = lax.axis_size("dp")
    shards = lax.axis_size("tensor")
    me = lax.axis_index("dp")
    rank_t = lax.axis_index("tensor")
    tokens, fp = arrivals.shape
    units = deal.shape[1]
    unit_rows = tokens // units
    slots = groups * MOST
    width = fp * shards
    qcols = w_query.shape[1]
    kv_heads = max(1, KVH // shards)
    kv_first = rank_t * KVH // shards
    cache_cols = 2 * KVH * HEAD // shards
    kvcols = 2 * HEAD * kv_heads
    cols = qcols + kvcols
    params = pltpu.CompilerParams(vmem_limit_bytes=VMEM_LIMIT)

    wo_full = lax.all_gather(w_out, "tensor", axis=0, tiled=True)

    dest_row = deal[0]
    target = dest_row // units
    unit_index = jnp.arange(units, dtype=jnp.int32)
    earlier = unit_index[:, None] > unit_index[None, :]
    rank = jnp.sum(jnp.logical_and(earlier, target[:, None] == target[None, :]), axis=1)
    slot = (target * MOST + rank).astype(jnp.int32)
    slot_index = jnp.arange(slots, dtype=jnp.int32)
    hot = slot[None, :] == slot_index[:, None]
    src = jnp.sum(jnp.where(hot, unit_index[None, :], 0), axis=1).astype(jnp.int32)

    slot_pos = jnp.sum(jnp.where(hot, dest_row[None, :] % units + 1, 0), axis=1) - 1
    pos = jnp.broadcast_to(
        jnp.pad(slot_pos.astype(jnp.int32).reshape(groups, 1, MOST), ((0, 0), (0, 0), (0, LANES - MOST))),
        (groups, 8, LANES),
    )

    ones = jnp.ones((HEAD,), jnp.float32)
    hgain = jnp.concatenate(
        [jnp.tile(query_gain, qcols // HEAD)]
        + [jnp.concatenate([key_gain, ones])] * kv_heads
    )[None, :]
    normed_cols = jnp.concatenate(
        [jnp.ones((qcols,), jnp.float32)]
        + [jnp.concatenate([ones, jnp.zeros((HEAD,), jnp.float32)])] * kv_heads
    )[None, :]
    lane = jnp.arange(LANES, dtype=jnp.int32)
    mean_mat = jnp.where(
        lane[:, None] // HEAD == lane[None, :] // HEAD, 1.0 / HEAD, 0.0
    ).astype(jnp.bfloat16)

    const = lambda shape: pl.BlockSpec(
        shape, lambda i: (0,) * len(shape), pipeline_mode=pl.Buffered(1)
    )
    held, xg, rpos = pl.pallas_call(
        functools.partial(qkv_kernel, groups, shards),
        in_specs=[VMEM, ANY, VMEM, ANY, ANY, VMEM, VMEM, VMEM],
        out_specs=[VMEM] * 3,
        out_shape=[
            jax.ShapeDtypeStruct((tokens, cols), jnp.bfloat16),
            jax.ShapeDtypeStruct((shards, tokens, fp), jnp.bfloat16),
            jax.ShapeDtypeStruct((groups, 8, LANES), jnp.int32),
        ],
        scratch_shapes=[
            pltpu.VMEM((TILE, width), jnp.bfloat16),
            pltpu.VMEM((width, qcols), jnp.bfloat16),
            pltpu.VMEM((width, kvcols), jnp.bfloat16),
            pltpu.SemaphoreType.DMA((2,)),
            pltpu.SemaphoreType.DMA((tokens // TILE,)),
            pltpu.SemaphoreType.DMA((shards - 1, tokens // TILE)),
            pltpu.SemaphoreType.DMA((shards - 1, tokens // TILE)),
            pltpu.SemaphoreType.DMA((groups - 1,)),
            pltpu.SemaphoreType.DMA((groups - 1,)),
        ],
        compiler_params=pltpu.CompilerParams(
            vmem_limit_bytes=VMEM_LIMIT, collective_id=0, has_side_effects=True
        ),
        name="qkv",
    )(pos, arrivals, attn_gain[None, :], w_query, w_keyval, hgain, normed_cols, mean_mat)

    packed = move_units(src, held, slots, unit_rows)

    recv_pos = rpos[:, 0, :MOST].reshape(-1)
    fill = recv_pos[None, :] == unit_index[:, None]
    slot_of = jnp.sum(jnp.where(fill, slot_index[None, :], 0), axis=1).astype(jnp.int32)
    pos_of = jnp.maximum(recv_pos, 0).astype(jnp.int32)

    received = lax.all_to_all(
        packed.reshape(groups, MOST * unit_rows, cols), "dp", split_axis=0, concat_axis=0, tiled=True
    ).reshape(slots * unit_rows, cols)

    starts = segment_starts(seg_ids[0])
    half = HEAD // 2
    inverse = THETA ** (-jnp.arange(half, dtype=jnp.float32) * 2.0 / HEAD)
    positions = jnp.arange(tokens, dtype=jnp.int32) - starts
    angles = positions.astype(jnp.float32)[:, None] * inverse[None, :]
    cosine, sine = jnp.cos(angles), jnp.sin(angles)
    cosq = jnp.tile(cosine, (1, 4))
    sinq = jnp.tile(sine, (1, 4))
    coskv = jnp.concatenate([cosine, cosine, jnp.ones((tokens, HEAD), jnp.float32)], axis=1)
    sinkv = jnp.concatenate([sine, sine, jnp.zeros((tokens, HEAD), jnp.float32)], axis=1)
    inn, out_l = lane[:, None], lane[None, :]
    rot = jnp.where(
        jnp.logical_and(out_l % HEAD < half, inn == out_l + half),
        -1.0,
        jnp.where(jnp.logical_and(out_l % HEAD >= half, inn == out_l - half), 1.0, 0.0),
    ).astype(jnp.bfloat16)

    npages = tokens // PAGE
    kv_pages, back = pl.pallas_call(
        functools.partial(attention_kernel, unit_rows, slots, qcols),
        in_specs=[SMEM] * 3 + [VMEM] * 7,
        out_specs=[VMEM] * 2,
        out_shape=[
            jax.ShapeDtypeStruct((npages, PAGE, kvcols), jnp.bfloat16),
            jax.ShapeDtypeStruct((slots * unit_rows, qcols), jnp.bfloat16),
        ],
        scratch_shapes=[
            pltpu.VMEM((tokens, cols), jnp.bfloat16),
            pltpu.VMEM((tokens, qcols), jnp.bfloat16),
            pltpu.VMEM((tokens, kvcols), jnp.bfloat16),
            pltpu.VMEM((tokens, qcols), jnp.bfloat16),
        ],
        compiler_params=params,
        name="attention",
    )(slot_of, pos_of, page_table[0], received, cosq, sinq, coskv, sinkv, starts[:, None], rot)

    if cache_cols < kvcols:
        offset = rank_t * cache_cols - kv_first * 2 * HEAD
        kv_pages = lax.dynamic_slice_in_dim(kv_pages, offset, cache_cols, 2)

    returned = lax.all_to_all(
        back.reshape(groups, MOST * unit_rows, qcols), "dp", split_axis=0, concat_axis=0, tiled=True
    ).reshape(slots * unit_rows, qcols)
    own_att = move_units(slot, returned, units, unit_rows)

    ff = w_gate.shape[1]
    ft = next(t for t in (512, 256, 128) if ff % t == 0)
    nf = ff // ft
    dt = min(512, fp)
    nd = width // dt
    away = nd - fp // dt
    result = pl.pallas_call(
        functools.partial(ffn_kernel, nf, shards),
        grid=(nf + nd,),
        in_specs=[
            const((shards, tokens, fp)),
            const((tokens, qcols)),
            const((qcols * shards, width)),
            const((1, width)),
            pl.BlockSpec((width, ft), lambda i: (0, jnp.minimum(i, nf - 1))),
            pl.BlockSpec((width, ft), lambda i: (0, jnp.minimum(i, nf - 1))),
            ANY,
        ],
        out_specs=pl.BlockSpec((tokens, fp), lambda i: (0, 0), pipeline_mode=pl.Buffered(1)),
        out_shape=jax.ShapeDtypeStruct((tokens, fp), jnp.bfloat16),
        scratch_shapes=[
            pltpu.VMEM((shards, tokens, qcols), jnp.bfloat16),
            pltpu.VMEM((tokens, fp), jnp.bfloat16),
            pltpu.VMEM((tokens, width), jnp.bfloat16),
            pltpu.VMEM((tokens, ff), jnp.bfloat16),
            pltpu.VMEM((nd, ff, dt), jnp.bfloat16),
            pltpu.VMEM((away, tokens, dt), jnp.bfloat16),
            pltpu.VMEM((away, tokens, dt), jnp.bfloat16),
            pltpu.SemaphoreType.DMA((nd,)),
            pltpu.SemaphoreType.DMA((shards - 1, tokens // TILE)),
            pltpu.SemaphoreType.DMA((shards - 1, tokens // TILE)),
            pltpu.SemaphoreType.DMA((away,)),
            pltpu.SemaphoreType.DMA((away,)),
        ],
        compiler_params=pltpu.CompilerParams(
            vmem_limit_bytes=VMEM_LIMIT, collective_id=1, has_side_effects=True
        ),
        name="ffn",
    )(xg, own_att, wo_full, ffn_gain[None, :], w_gate, w_up, w_down)
    return (result, kv_pages)


def solution(mesh):
    return jax.shard_map(
        on_device,
        mesh=mesh,
        in_specs=(
            P("dp", "tensor"),
            P("dp", None),
            P("dp", None),
            P("dp", None),
            P(),
            P(None, "tensor"),
            P(),
            P(),
            P(),
            P("tensor", None),
            P(),
            P(None, "tensor"),
            P(None, "tensor"),
            P("tensor", None),
        ),
        out_specs=(P("dp", "tensor"), P("dp", None, "tensor")),
        check_vma=False,
    )
```
